256 devices in a mesh: row: 8 (over z), col: 32 (over y, x, core).
Axes of the slice: x: 4, y: 4, z: 8, core: 2. Of those that a mesh axis runs over, the one named last changes fastest.
Arguments:
- psi: bfloat16 [1024, 128, 128], P(('row', 'col')), may hold values from -6 to 6
- right_env: bfloat16 [1024, 128, 32, 128], P(('row', 'col')), may hold values from -0.5 to 0.5
- left_env: bfloat16 [8, 128, 32, 128], P('row'), may hold values from -0.09375 to 0.09375
- env_index: int32 [8192], P(('row', 'col')), may hold values from 0 to 7
- source_block: int32 [8192], P(('row', 'col')), may hold values from 0 to 3
- target_slot: int32 [8192], P(('row', 'col')), may hold values from 0 to 63, as said below
- target_block: int32 [8192], P(('row', 'col')), may hold values from 0 to 3
Outputs:
- psi_next: bfloat16 [1024, 128, 128], P(('row', 'col'))
The draws below stay inside these ranges and needn't reach their ends.
Inputs may be any that keep to these rules, and one draw needn't show every extreme that they name: `target_slot`: on each device's 32 pairs the entries are distinct; entry s is slot s % 2 toward col index s // 2. In every row one col index, drawn from the seed, receives all 2 slots from every device of that row. Every device's list holds slot 0 and slot 32 * 2 - 1.
All inputs are finite; a program needn't handle non-finite values.
Results may differ from the reference program's by a relative error of at most 0.01.
Values may be sent and summed in bfloat16 or wider, within the bound.
No kernel may reach another device: no remote copies, remote signals or barrier semaphores. Data moves between devices by JAX's collectives and lax.ppermute only.
A program may use at most 128 MiB of HBM per device.

```python
import jax
import jax.numpy as jnp
from jax import lax

BT = 128
W = 32
NB_DEV = 4
NP_DEV = 32
NBLK = 1024
ENVS = 8
NPAIR = 8192
CAP = 2
N_ROW = 8
N_COL = 32


def draw_target_slot(key, part):
    slots = N_COL * CAP
    hot = jax.random.randint(jax.random.fold_in(key, 1), (N_ROW,), 0, N_COL)
    hot_device = jnp.repeat(hot, N_COL)
    keys = jax.random.split(jax.random.fold_in(key, 2), N_ROW * N_COL)

    def one_device(device_key, hot_col):
        order = jax.random.permutation(device_key, slots)
        owner = order // CAP
        ends = (order == 0) | (order == slots - 1)
        priority = jnp.where(owner == hot_col, -2, jnp.where(ends, -1, jnp.arange(slots)))
        ranked = jnp.argsort(priority, stable=True)
        return order[ranked][:NP_DEV]
    return jax.vmap(one_device)(keys, hot_device).reshape(-1).astype(jnp.int32)


def plant(values, stream_key, smallest, high):
    place = [jax.random.randint(jax.random.fold_in(stream_key, axis), (), 0, length) for axis, length in enumerate(values.shape)]
    widest = values.shape.index(max(values.shape))
    next_to = place[:widest] + [(place[widest] + 1) % values.shape[widest]] + place[widest + 1:]
    return values.at[tuple(place)].set(smallest).at[tuple(next_to)].set(high)


def levels(stream_key, dims, cuts, low, high):
    def one(axis_at, shards_of):
        draws = jax.random.uniform(jax.random.fold_in(jax.random.fold_in(stream_key, 6), axis_at), (shards_of,), jnp.float32, low / len(cuts), high / len(cuts))
        return jnp.repeat(jnp.exp(draws), dims[axis_at] // shards_of).reshape((-1,) + (1,) * (len(dims) - axis_at - 1))

    loudness = one(*cuts[0])
    for cut in cuts[1:]:
        loudness = loudness * one(*cut)
    return loudness


def normal_values(key, shape, width, most, pieces=(), kind=jnp.bfloat16):
    drawn = width * jax.random.normal(key, shape, jnp.float32)
    if pieces:
        drawn = drawn * levels(key, shape, pieces, -0.22, 0.18)
    return jnp.clip(drawn, -most, most).astype(kind)


def setup_inputs(seed: int = 0) -> dict:
    seeds = jax.random.split(jax.random.key(seed), 8)
    psi = normal_values(seeds[0], (NBLK, BT, BT), 1.0, 6.0, ((0, 256),))
    right_env = normal_values(seeds[1], (NBLK, BT, W, BT), BT ** -0.5, 0.5, ((0, 256),))
    left_env = normal_values(seeds[2], (ENVS, BT, W, BT), (W * BT) ** -0.5, 0.09375, ((0, 8),))
    env_index = plant(jax.random.randint(seeds[3], (NPAIR,), 0, ENVS), jax.random.fold_in(seeds[3], 1), 0, ENVS - 1).astype(jnp.int32)
    source_block = plant(jax.random.randint(seeds[4], (NPAIR,), 0, NB_DEV), jax.random.fold_in(seeds[4], 1), 0, NB_DEV - 1).astype(jnp.int32)
    target_slot = draw_target_slot(jax.random.fold_in(seeds[7], 71), 0)
    target_block = plant(jax.random.randint(seeds[6], (NPAIR,), 0, NB_DEV), jax.random.fold_in(seeds[6], 1), 0, NB_DEV - 1).astype(jnp.int32)
    return dict(psi=psi, right_env=right_env, left_env=left_env, env_index=env_index, source_block=source_block, target_slot=target_slot, target_block=target_block)


def reference(psi, right_env, left_env, env_index, source_block, target_slot, target_block):
    state = psi
    devices = N_ROW * N_COL
    for step in range(2):
        def per_device(total, device):
            row_index = device // N_COL
            blocks = lax.dynamic_slice_in_dim(state, device * NB_DEV, NB_DEV, 0)
            renv = lax.dynamic_slice_in_dim(right_env, device * NB_DEV, NB_DEV, 0)
            product = jnp.einsum('bkl,blwj->bkwj', blocks.astype(jnp.float32), renv.astype(jnp.float32)).astype(jnp.bfloat16)
            env_ids = lax.dynamic_slice_in_dim(env_index, device * NP_DEV, NP_DEV, 0)
            src_ids = lax.dynamic_slice_in_dim(source_block, device * NP_DEV, NP_DEV, 0)
            slot_ids = lax.dynamic_slice_in_dim(target_slot, device * NP_DEV, NP_DEV, 0)
            blk_ids = lax.dynamic_slice_in_dim(target_block, device * NP_DEV, NP_DEV, 0)
            left = left_env[env_ids].astype(jnp.float32)
            right = product[src_ids].astype(jnp.float32)
            partial_value = jnp.einsum('pawk,pkwj->paj', left, right).astype(jnp.bfloat16)
            dest = ((row_index * N_COL + slot_ids // CAP) * NB_DEV + blk_ids).astype(jnp.int32)
            total = total.at[dest].add(partial_value.astype(jnp.float32))
            return total, None

        total, _ = lax.scan(per_device, jnp.zeros((NBLK, BT, BT), jnp.float32), jnp.arange(devices, dtype=jnp.int32))
        state = (state.astype(jnp.float32) - 0.3 * total).astype(jnp.bfloat16)
    return state
```

```python
import jax
import jax.numpy as jnp
from jax import lax
from jax.experimental import pallas as pl
from jax.experimental.pallas import tpu as pltpu
from jax.sharding import PartitionSpec as P

step_size = 0.3
NX = 4
NY = 4

other_core = [(i, i ^ 1) for i in range(2 * NX * NY)]


def col_of(y, x, core):
    return (y * NX + x) * 2 + core


x_lines = [[[col_of(y, x, c) for x in range(NX)] for y in range(NY)] for c in range(2)]
y_lines = [[[col_of(y, x, c) for y in range(NY)] for x in range(NX)] for c in range(2)]
first_groups = x_lines[0] + y_lines[1]
second_groups = y_lines[0] + x_lines[1]


def contract_kernel(
    pairs, own_rows, other_rows, right_own, right_other, left, out,
    right_v, left_v, state, product, partial, right_sem, left_sem,
):
    nb, side, wide = right_own.shape
    half = side // 2
    blocks = 2 * nb
    pair_count = pairs.shape[1]
    core = pairs[3, 0]
    copies = []
    for b in range(blocks):
        src = right_own.at[b] if b < nb else right_other.at[b - nb]
        copies.append(pltpu.make_async_copy(src, right_v.at[b], right_sem.at[b]))
    left_copy = pltpu.make_async_copy(left, left_v, left_sem)
    for c in copies:
        c.start()
    left_copy.start()
    mine = pl.multiple_of(core * half, half)
    theirs = pl.multiple_of((1 - core) * half, half)
    state[:, pl.ds(mine, half), :] = own_rows[...]
    state[:, pl.ds(theirs, half), :] = other_rows[...]
    out[...] = jnp.zeros_like(out)
    step = 512
    for b in range(blocks):
        copies[b].wait()
        at = core * nb + b if b < nb else (1 - core) * nb + b - nb
        s = state[at]
        for n in range(wide // step):
            r = jnp.dot(
                s, right_v[b, :, n * step:(n + 1) * step], preferred_element_type=jnp.float32
            ).astype(jnp.bfloat16)
            for q in range(step // side):
                w = n * (step // side) + q
                product[w * side:(w + 1) * side, b * side:(b + 1) * side] = r[
                    :, q * side:(q + 1) * side
                ]
    left_copy.wait()
    for n in range(blocks // 2):
        r = jnp.dot(
            left_v[...], product[:, n * 2 * side:(n + 1) * 2 * side],
            preferred_element_type=jnp.float32,
        ).astype(jnp.bfloat16)
        partial[2 * n] = r[:, :side]
        partial[2 * n + 1] = r[:, side:]

    def place(p, carry):
        rows = pl.multiple_of(pairs[0, p] * half, half)
        to = pairs[2, p]
        value = partial[pairs[1, p], pl.ds(rows, half), :].astype(jnp.float32)
        out[to] = (out[to].astype(jnp.float32) + value).astype(jnp.bfloat16)
        return carry

    lax.fori_loop(0, pair_count, place, 0)


def contract(pairs, own_rows, other_rows, right_own, right_other, left):
    nb, side, wide = right_own.shape
    blocks = 2 * nb
    dests = NX * NY * blocks
    vmem = pl.BlockSpec(memory_space=pltpu.VMEM)
    anywhere = pl.BlockSpec(memory_space=pl.ANY)
    flops = 2 * (blocks * side * side * wide + left.shape[0] * wide * blocks * side)
    moved = 2 * (2 * right_own.size + left.size + dests * side * side // 2)
    return pl.pallas_call(
        contract_kernel,
        out_shape=jax.ShapeDtypeStruct((dests, side // 2, side), jnp.bfloat16),
        in_specs=[
            pl.BlockSpec(memory_space=pltpu.SMEM), vmem, vmem, anywhere, anywhere, anywhere
        ],
        out_specs=vmem,
        scratch_shapes=[
            pltpu.VMEM((blocks, side, wide), jnp.bfloat16),
            pltpu.VMEM(left.shape, jnp.bfloat16),
            pltpu.VMEM((blocks, side, side), jnp.bfloat16),
            pltpu.VMEM((wide, blocks * side), jnp.bfloat16),
            pltpu.VMEM((blocks, left.shape[0], side), jnp.bfloat16),
            pltpu.SemaphoreType.DMA((blocks,)),
            pltpu.SemaphoreType.DMA,
        ],
        compiler_params=pltpu.CompilerParams(vmem_limit_bytes=48 * 1024 * 1024),
        cost_estimate=pl.CostEstimate(flops=flops, bytes_accessed=moved, transcendentals=0),
        name="contract",
    )(pairs, own_rows, other_rows, right_own, right_other, left)


def on_device(psi, right_env, left_env, env_index, source_block, target_slot, target_block):
    nb, side, width, _ = right_env.shape
    half = side // 2
    blocks = 2 * nb
    core = lax.axis_index("col") % 2

    def swap(a):
        return lax.ppermute(a, "col", other_core)

    own_left = lax.dynamic_slice_in_dim(left_env[0], core * half, half, 0)
    left = lax.all_gather(
        own_left.reshape(half, width * side), "row", axis=0, tiled=True
    )

    owner = target_slot // 2
    y, x, c = owner // (2 * NX), (owner // 2) % NX, owner % 2
    x_first = ((x * NY + y) * 2 + c) * nb + target_block
    y_first = ((y * NX + x) * 2 + c) * nb + target_block
    lists = jnp.stack([env_index, source_block, x_first, y_first])
    theirs = swap(lists)
    both = jnp.concatenate([lists, theirs + jnp.array([[0], [nb], [0], [0]], jnp.int32)], axis=1)
    to = jnp.where(core == 0, both[2], both[3])
    pairs = jnp.stack([both[0], both[1], to, jnp.full_like(to, core)])

    right_own = right_env.reshape(nb, side, width * side)
    right_other = swap(right_own)
    psi_other = swap(psi)
    lower = jnp.where(core == 0, psi, psi_other)
    upper = jnp.where(core == 0, psi_other, psi)
    state = jnp.concatenate([lower, upper], axis=0)
    own_rows = jnp.where(core == 0, state[:, :half], state[:, half:])
    other_rows = jnp.where(core == 0, state[:, half:], state[:, :half])
    for step in range(2):
        sums = contract(pairs, own_rows, other_rows, right_own, right_other, left)
        got = lax.all_to_all(
            sums.reshape(4, 4 * blocks, half, side), "col", 0, 0,
            axis_index_groups=first_groups, tiled=True,
        )
        line = jnp.sum(got.astype(jnp.float32), axis=0).astype(jnp.bfloat16)
        got = lax.all_to_all(
            line.reshape(4, blocks, half, side), "col", 0, 0,
            axis_index_groups=second_groups, tiled=True,
        )
        gradient = jnp.sum(got.astype(jnp.float32), axis=0)
        own_rows = (own_rows.astype(jnp.float32) - step_size * gradient).astype(jnp.bfloat16)
        if step == 0:
            other_rows = swap(own_rows)
    keep = jnp.where(core == 0, own_rows[:nb], own_rows[nb:])
    send = jnp.where(core == 0, own_rows[nb:], own_rows[:nb])
    come = swap(send)
    top = jnp.where(core == 0, keep, come)
    bottom = jnp.where(core == 0, come, keep)
    return jnp.concatenate([top, bottom], axis=1)


def solution(mesh):
    placed = (
        P(("row", "col"), None, None),
        P(("row", "col"), None, None, None),
        P("row", None, None, None),
        P(("row", "col")),
        P(("row", "col")),
        P(("row", "col")),
        P(("row", "col")),
    )
    return jax.shard_map(
        on_device,
        mesh=mesh,
        in_specs=placed,
        out_specs=P(("row", "col"), None, None),
        check_vma=False,
    )
```

```python
import jax
import jax.numpy as jnp
from jax import lax
from jax.experimental import pallas as pl
from jax.experimental.pallas import tpu as pltpu
from jax.sharding import PartitionSpec as P

step_size = 0.3
NZ, NY, NX = 8, 4, 4
axes = ("row", "col")

far = (2, -2, 3, -3, 4)
thirds = 3
third_w = 11
near = 3


def device(z, y, x, c):
    return ((z % NZ * NY + y % NY) * NX + x % NX) * 2 + c


def permutation(to):
    return [
        (device(z, y, x, c), device(*to(z, y, x, c)))
        for z in range(NZ) for y in range(NY) for x in range(NX) for c in range(2)
    ]


swap_cores = permutation(lambda z, y, x, c: (z, y, x, 1 - c))


def first(d):
    return permutation(lambda z, y, x, c: (z, y, x + d, c) if c == 0 else (z, y + d, x, c))


def second(d):
    return permutation(lambda z, y, x, c: (z, y + d, x, c) if c == 0 else (z, y, x + d, c))


def along_z(d):
    return permutation(lambda z, y, x, c: (z + d, y, x, c))


def fetch_place(z, y, x, c):
    group = min((y * NX + x) // thirds, len(far) - 1)
    d = far[group] if c == 0 else -far[group]
    return z - d, y, x, c


fetch_far = permutation(fetch_place)
shifts = (1, 2, -1)


def send(a, perm):
    return lax.ppermute(a, axes, perm)


def table(values, index):
    out = jnp.full_like(index, values[0])
    for k, v in enumerate(values[1:], 1):
        out = jnp.where(index == k, v, out)
    return out


vmem = pl.BlockSpec(memory_space=pltpu.VMEM)
smem = pl.BlockSpec(memory_space=pltpu.SMEM)


def params(mib):
    return pltpu.CompilerParams(vmem_limit_bytes=mib * 1024 * 1024)


def multiply_state(core, own_rows, other_rows, right_own, right_other, state, product):
    nb, side, wide = right_own.shape
    half = side // 2
    mine = pl.multiple_of(core * half, half)
    theirs = pl.multiple_of((1 - core) * half, half)
    state[:, pl.ds(mine, half), :] = own_rows[...]
    state[:, pl.ds(theirs, half), :] = other_rows[...]
    step = 512
    for b in range(2 * nb):
        at = core * nb + b if b < nb else (1 - core) * nb + b - nb
        right = right_own.at[b] if b < nb else right_other.at[b - nb]
        s = state[at]
        for n in range(wide // step):
            r = jnp.dot(
                s, right[:, n * step:(n + 1) * step], preferred_element_type=jnp.float32
            ).astype(jnp.bfloat16)
            for q in range(step // side):
                w = n * (step // side) + q
                product[w * side:(w + 1) * side, b * side:(b + 1) * side] = r[
                    :, q * side:(q + 1) * side
                ]


def multiply_left(pairs, left, product, partial, total, outs):
    half, side = total.shape[1:]
    wide = product.shape[0]
    rows = partial.shape[1]
    total[...] = jnp.zeros_like(total)
    for n in range(partial.shape[0] // 2):
        r = jnp.dot(
            left[:rows, :wide], product[:, n * 2 * side:(n + 1) * 2 * side],
            preferred_element_type=jnp.float32,
        ).astype(jnp.bfloat16)
        partial[2 * n] = r[:, :side]
        partial[2 * n + 1] = r[:, side:]

    def place(p, carry):
        at = pl.multiple_of(pairs[0, p] * half, half)
        to = pairs[2, p]
        value = partial[pairs[1, p], pl.ds(at, half), :].astype(jnp.float32)
        total[to] = (total[to].astype(jnp.float32) + value).astype(jnp.bfloat16)
        return carry

    lax.fori_loop(0, pairs.shape[1], place, 0, unroll=4)
    count = outs[0].shape[0]
    for i, out in enumerate(outs):
        out[...] = total[i * count:(i + 1) * count]


def product_kernel(pairs, own_rows, other_rows, right_own, right_other, product, state):
    multiply_state(pairs[3, 0], own_rows, other_rows, right_own, right_other, state, product)


def first_kernel(
    pairs, places, own, below, above, part0, part1, part2, part3, product,
    out0, out1, out2, out3, left, partial, total, sems, near_sems,
):
    half = own.shape[0]
    copies = []
    for i, ref in enumerate((own, below, above)):
        copies.append(
            pltpu.make_async_copy(
                ref, left.at[i * half:(i + 1) * half, 0:own.shape[1]], near_sems.at[i]
            )
        )
    for i, ref in enumerate((part0, part1, part2, part3)):
        for j in range(4):
            row = pl.multiple_of(places[0, i * 4 + j], half)
            column = pl.multiple_of(places[1, i * 4 + j], 128)
            copies.append(
                pltpu.make_async_copy(
                    ref.at[j], left.at[pl.ds(row, half), pl.ds(column, ref.shape[2])],
                    sems.at[i * 4 + j],
                )
            )
    for c in copies:
        c.start()
    for c in copies:
        c.wait()
    multiply_left(pairs, left, product, partial, total, (out0, out1, out2, out3))


def second_kernel(
    pairs, own_rows, other_rows, right_own, right_other, left,
    out0, out1, out2, out3, state, product, partial, total,
):
    multiply_state(pairs[3, 0], own_rows, other_rows, right_own, right_other, state, product)
    multiply_left(pairs, left, product, partial, total, (out0, out1, out2, out3))


def on_device(psi, right_env, left_env, env_index, source_block, target_slot, target_block):
    nb, side, width, _ = right_env.shape
    half = side // 2
    blocks = 2 * nb
    envs = NZ
    wide = width * side
    third = third_w * side
    bf16, f32 = jnp.bfloat16, jnp.float32
    z = lax.axis_index("row")
    col = lax.axis_index("col")
    core, x, y = col % 2, col // 2 % NX, col // (2 * NX)
    lower = core == 0
    chip = y * NX + x

    own = lax.dynamic_slice_in_dim(left_env[0], core * half, half, 0).reshape(half, wide)
    padded = jnp.pad(own, ((0, 0), (0, thirds * third - wide)))
    mine = lax.dynamic_slice_in_dim(padded, chip % thirds * third, third, 1)
    held = send(mine, fetch_far)
    env_index, target_slot, right_env, _ = lax.optimization_barrier(
        (env_index, target_slot, right_env, mine)
    )
    offset = (env_index - z) % envs
    slot_lower = table([0, 2, 3, 5, 7, 6, 4, 1], offset)
    slot_upper = table([0, 2, 4, 6, 7, 5, 3, 1], offset)
    owner = target_slot // 2
    to_y, to_x, to_c = owner // (2 * NX), owner // 2 % NX, owner % 2
    ry, rx = (to_y - y) % NY, (to_x - x) % NX
    block = to_c * nb + target_block
    x_first = (rx * 4 + ry) * blocks + block
    y_first = (ry * 4 + rx) * blocks + block
    lists = jnp.stack([slot_lower, slot_upper, source_block, x_first, y_first])
    right_own = right_env.reshape(nb, side, wide)
    psi_other = send(psi, swap_cores)
    their_lists = send(lists, swap_cores)
    held, own, right_own, psi_other, their_lists = lax.optimization_barrier(
        (held, own, right_own, psi_other, their_lists)
    )
    right_other = send(right_own, swap_cores)
    below = send(own, along_z(1))
    above = send(own, along_z(-1))
    line = jnp.stack([held] + [send(held, first(d)) for d in shifts])
    line, right_other = lax.optimization_barrier((line, right_other))
    last_line, below, above = lax.optimization_barrier((line, below, above))
    parts = [line] + [send(last_line if d < 0 else line, second(d)) for d in shifts]

    back = jnp.array([0, -1, -2, 1], jnp.int32)
    by_first, by_second = back[None, :], back[:, None]
    px = (x + jnp.where(lower, by_first, by_second)) % NX
    py = (y + jnp.where(lower, by_second, by_first)) % NY
    at = (py * NX + px).reshape(-1)
    places = jnp.stack([(near + at // thirds) * half, at % thirds * third])

    theirs = their_lists + jnp.array([[0], [0], [nb], [0], [0]], jnp.int32)
    both = jnp.concatenate([lists, theirs], axis=1)
    pairs = jnp.stack([
        jnp.where(lower, both[0], both[1]), both[2],
        jnp.where(lower, both[3], both[4]), jnp.broadcast_to(core, both[2].shape),
    ])

    state = jnp.concatenate(
        [jnp.where(lower, psi, psi_other), jnp.where(lower, psi_other, psi)], axis=0
    )
    own_rows = jnp.where(lower, state[:, :half], state[:, half:])
    other_rows = jnp.where(lower, state[:, half:], state[:, :half])

    pair_count = pairs.shape[1]
    left_shape = ((envs + 1) * half, thirds * third)
    sums_shape = [jax.ShapeDtypeStruct((4 * blocks, half, side), bf16)] * 4
    state_scratch = pltpu.VMEM((blocks, side, side), bf16)
    product_scratch = pltpu.VMEM((wide, blocks * side), bf16)
    left_scratch = [
        pltpu.VMEM((blocks, envs * half, side), bf16),
        pltpu.VMEM((16 * blocks, half, side), bf16),
    ]
    state_flops = 2 * blocks * side * side * wide
    left_flops = 2 * envs * half * wide * blocks * side

    product = pl.pallas_call(
        product_kernel,
        out_shape=jax.ShapeDtypeStruct((wide, blocks * side), bf16),
        in_specs=[smem] + [vmem] * 4,
        out_specs=vmem,
        scratch_shapes=[state_scratch],
        compiler_params=params(8),
        cost_estimate=pl.CostEstimate(flops=state_flops, bytes_accessed=0, transcendentals=0),
        name="product",
    )(pairs, own_rows, other_rows, right_own, right_other)

    for step in range(2):
        if step == 0:
            *sums, left = pl.pallas_call(
                first_kernel,
                out_shape=sums_shape + [jax.ShapeDtypeStruct(left_shape, bf16)],
                in_specs=[smem] * 2 + [vmem] * 8,
                out_specs=[vmem] * 5,
                scratch_shapes=left_scratch + [
                    pltpu.SemaphoreType.DMA((16,)), pltpu.SemaphoreType.DMA((near,))
                ],
                compiler_params=params(12),
                cost_estimate=pl.CostEstimate(
                    flops=left_flops, bytes_accessed=0, transcendentals=0
                ),
                name="contract_first",
            )(pairs, places, own, below, above, *parts, product)
        else:
            sums = pl.pallas_call(
                second_kernel,
                out_shape=sums_shape,
                in_specs=[smem] + [vmem] * 5,
                out_specs=[vmem] * 4,
                scratch_shapes=[state_scratch, product_scratch] + left_scratch,
                compiler_params=params(24),
                cost_estimate=pl.CostEstimate(
                    flops=left_flops + state_flops, bytes_accessed=0, transcendentals=0
                ),
                name="contract_second",
            )(pairs, own_rows, other_rows, right_own, right_other, left)
        got = [send(sums[k + 1], first(d)) for k, d in enumerate(shifts)]
        summed = sums[0].astype(f32)
        for g in got:
            summed = summed + g.astype(f32)
        summed = summed.astype(bf16).reshape(4, blocks, half, side)
        got = [send(summed[k + 1], second(d)) for k, d in enumerate(shifts)]
        gradient = summed[0].astype(f32)
        for g in got:
            gradient = gradient + g.astype(f32)
        own_rows = (own_rows.astype(f32) - step_size * gradient).astype(bf16)
        if step == 0:
            other_rows = send(own_rows, swap_cores)
    keep = jnp.where(lower, own_rows[:nb], own_rows[nb:])
    give = jnp.where(lower, own_rows[nb:], own_rows[:nb])
    come = send(give, swap_cores)
    return jnp.concatenate(
        [jnp.where(lower, keep, come), jnp.where(lower, come, keep)], axis=1
    )


def solution(mesh):
    placed = (
        P(("row", "col"), None, None),
        P(("row", "col"), None, None, None),
        P("row", None, None, None),
        P(("row", "col")),
        P(("row", "col")),
        P(("row", "col")),
        P(("row", "col")),
    )
    return jax.shard_map(
        on_device,
        mesh=mesh,
        in_specs=placed,
        out_specs=P(("row", "col"), None, None),
        check_vma=False,
    )
```

```python
import jax
import jax.numpy as jnp
from jax import lax
from jax.experimental import pallas as pl
from jax.experimental.pallas import tpu as pltpu
from jax.sharding import PartitionSpec as P

step_size = 0.3
NZ, NY, NX = 8, 4, 4
axes = ("row", "col")

far = (2, -2, 3, -3, 4)
thirds = 3
third_w = 11
near = 3


def device(z, y, x, c):
    return ((z % NZ * NY + y % NY) * NX + x % NX) * 2 + c


def permutation(to):
    return [
        (device(z, y, x, c), device(*to(z, y, x, c)))
        for z in range(NZ) for y in range(NY) for x in range(NX) for c in range(2)
    ]


swap_cores = permutation(lambda z, y, x, c: (z, y, x, 1 - c))


def first(d):
    return permutation(lambda z, y, x, c: (z, y, x + d, c) if c == 0 else (z, y + d, x, c))


def second(d):
    return permutation(lambda z, y, x, c: (z, y + d, x, c) if c == 0 else (z, y, x + d, c))


def along_z(d):
    return permutation(lambda z, y, x, c: (z + d, y, x, c))


def fetch_place(z, y, x, c):
    group = min((y * NX + x) // thirds, len(far) - 1)
    d = far[group] if c == 0 else -far[group]
    return z - d, y, x, c


fetch_far = permutation(fetch_place)
shifts = (1, 2, -1)


def send(a, perm):
    return lax.ppermute(a, axes, perm)


def table(values, index):
    out = jnp.full_like(index, values[0])
    for k, v in enumerate(values[1:], 1):
        out = jnp.where(index == k, v, out)
    return out


vmem = pl.BlockSpec(memory_space=pltpu.VMEM)
smem = pl.BlockSpec(memory_space=pltpu.SMEM)
anywhere = pl.BlockSpec(memory_space=pl.ANY)


def params(mib):
    return pltpu.CompilerParams(vmem_limit_bytes=mib * 1024 * 1024)


def multiply_state(
    core, own_rows, other_rows, right_own, right_other, right_v, right_sems, state, product
):
    count, side, wide = right_own.shape
    copies = [
        pltpu.make_async_copy(right_other.at[b], right_v.at[b], right_sems.at[b])
        for b in range(count)
    ]
    for c in copies:
        c.start()
    half = side // 2
    blocks = state.shape[0]
    nb = blocks // 2
    mine = pl.multiple_of(core * half, half)
    theirs = pl.multiple_of((1 - core) * half, half)
    state[:, pl.ds(mine, half), :] = own_rows[...]
    state[:, pl.ds(theirs, half), :] = other_rows[...]
    step = 512
    for b in range(blocks):
        at = core * nb + b if b < nb else (1 - core) * nb + b - nb
        if b >= count:
            copies[b - count].wait()
        right = right_own.at[b] if b < count else right_v.at[b - count]
        s = state[at]
        for n in range(wide // step):
            r = jnp.dot(
                s, right[:, n * step:(n + 1) * step], preferred_element_type=jnp.float32
            ).astype(jnp.bfloat16)
            for q in range(step // side):
                w = n * (step // side) + q
                product[w * side:(w + 1) * side, b * side:(b + 1) * side] = r[
                    :, q * side:(q + 1) * side
                ]


def multiply_left(left, product, partial, start, stop):
    wide = product.shape[0]
    side = partial.shape[2]
    for n in range(partial.shape[0] // 2):
        r = jnp.dot(
            left[:, :wide], product[:, n * 2 * side:(n + 1) * 2 * side],
            preferred_element_type=jnp.float32,
        ).astype(jnp.bfloat16)
        partial[2 * n, start:stop] = r[:, :side]
        partial[2 * n + 1, start:stop] = r[:, side:]


def place_pairs(pairs, partial, total, outs):
    half = total.shape[1]

    def place(p, carry):
        at = pl.multiple_of(pairs[0, p] * half, half)
        to = pairs[2, p]
        value = partial[pairs[1, p], pl.ds(at, half), :].astype(jnp.float32)
        total[to] = (total[to].astype(jnp.float32) + value).astype(jnp.bfloat16)
        return carry

    lax.fori_loop(0, pairs.shape[1], place, 0, unroll=4)
    count = outs[0].shape[0]
    for i, out in enumerate(outs):
        out[...] = total[i * count:(i + 1) * count]


def product_kernel(
    core, own_rows, other_rows, right_own, right_other, own, below, above,
    product, partial, state, right_v, right_sems,
):
    multiply_state(
        core[0], own_rows, other_rows, right_own, right_other, right_v, right_sems, state, product
    )
    stacked = jnp.concatenate([own[...], below[...], above[...]], axis=0)
    multiply_left(stacked, product, partial, 0, stacked.shape[0])


def first_kernel(
    pairs, places, own, below, above, part0, part1, part2, part3, product, partial_near,
    out0, out1, out2, out3, left, partial, total, sems, near_sems,
):
    half, wide = own.shape
    near_rows = near * half
    rows = partial.shape[1]
    near_copies = [
        pltpu.make_async_copy(
            ref, left.at[i * half:(i + 1) * half, 0:wide], near_sems.at[i]
        )
        for i, ref in enumerate((own, below, above))
    ]
    copies = []
    for i, ref in enumerate((part0, part1, part2, part3)):
        for j in range(4):
            row = pl.multiple_of(places[0, i * 4 + j], half)
            column = pl.multiple_of(places[1, i * 4 + j], 128)
            copies.append(
                pltpu.make_async_copy(
                    ref.at[j], left.at[pl.ds(row, half), pl.ds(column, ref.shape[2])],
                    sems.at[i * 4 + j],
                )
            )
    for c in copies + near_copies:
        c.start()
    total[...] = jnp.zeros_like(total)
    partial[:, :near_rows] = partial_near[...]
    for c in copies + near_copies:
        c.wait()
    multiply_left(left.at[near_rows:rows], product, partial, near_rows, rows)
    place_pairs(pairs, partial, total, (out0, out1, out2, out3))


def second_kernel(
    pairs, own_rows, other_rows, right_own, right_other, left,
    out0, out1, out2, out3, state, right_v, right_sems, product, partial, total,
):
    rows = partial.shape[1]
    total[...] = jnp.zeros_like(total)
    multiply_state(
        pairs[3, 0], own_rows, other_rows, right_own, right_other, right_v, right_sems, state, product
    )
    multiply_left(left.at[:rows], product, partial, 0, rows)
    place_pairs(pairs, partial, total, (out0, out1, out2, out3))


def on_device(psi, right_env, left_env, env_index, source_block, target_slot, target_block):
    nb, side, width, _ = right_env.shape
    half = side // 2
    blocks = 2 * nb
    envs = NZ
    wide = width * side
    third = third_w * side
    bf16, f32 = jnp.bfloat16, jnp.float32
    z = lax.axis_index("row")
    col = lax.axis_index("col")
    core, x, y = col % 2, col // 2 % NX, col // (2 * NX)
    lower = core == 0
    chip = y * NX + x

    own = lax.dynamic_slice_in_dim(left_env[0], core * half, half, 0).reshape(half, wide)
    padded = jnp.pad(own, ((0, 0), (0, thirds * third - wide)))
    mine = lax.dynamic_slice_in_dim(padded, chip % thirds * third, third, 1)
    held = send(mine, fetch_far)
    env_index, target_slot, right_env, _ = lax.optimization_barrier(
        (env_index, target_slot, right_env, mine)
    )
    offset = (env_index - z) % envs
    slot_lower = table([0, 2, 3, 5, 7, 6, 4, 1], offset)
    slot_upper = table([0, 2, 4, 6, 7, 5, 3, 1], offset)
    owner = target_slot // 2
    to_y, to_x, to_c = owner // (2 * NX), owner // 2 % NX, owner % 2
    ry, rx = (to_y - y) % NY, (to_x - x) % NX
    block = to_c * nb + target_block
    x_first = (rx * 4 + ry) * blocks + block
    y_first = (ry * 4 + rx) * blocks + block
    lists = jnp.stack([slot_lower, slot_upper, source_block, x_first, y_first])
    right_own = right_env.reshape(nb, side, wide)
    psi_other = send(psi, swap_cores)
    their_lists = send(lists, swap_cores)
    held, own, right_own, psi_other, their_lists = lax.optimization_barrier(
        (held, own, right_own, psi_other, their_lists)
    )
    right_other = send(right_own, swap_cores)
    below = send(own, along_z(1))
    above = send(own, along_z(-1))
    line = jnp.stack([held] + [send(held, first(d)) for d in shifts])
    line, right_other = lax.optimization_barrier((line, right_other))
    last_line, below, above = lax.optimization_barrier((line, below, above))
    parts = [line] + [send(last_line if d < 0 else line, second(d)) for d in shifts]
    rights = (right_own, right_other)

    back = jnp.array([0, -1, -2, 1], jnp.int32)
    by_first, by_second = back[None, :], back[:, None]
    px = (x + jnp.where(lower, by_first, by_second)) % NX
    py = (y + jnp.where(lower, by_second, by_first)) % NY
    at = (py * NX + px).reshape(-1)
    places = jnp.stack([(near + at // thirds) * half, at % thirds * third])

    theirs = their_lists + jnp.array([[0], [0], [nb], [0], [0]], jnp.int32)
    both = jnp.concatenate([lists, theirs], axis=1)
    pairs = jnp.stack([
        jnp.where(lower, both[0], both[1]), both[2],
        jnp.where(lower, both[3], both[4]), jnp.broadcast_to(core, both[2].shape),
    ])

    state = jnp.concatenate(
        [jnp.where(lower, psi, psi_other), jnp.where(lower, psi_other, psi)], axis=0
    )
    own_rows = jnp.where(lower, state[:, :half], state[:, half:])
    other_rows = jnp.where(lower, state[:, half:], state[:, :half])

    pair_count = pairs.shape[1]
    left_shape = ((envs + 1) * half, thirds * third)
    sums_shape = [jax.ShapeDtypeStruct((4 * blocks, half, side), bf16)] * 4
    state_scratch = [
        pltpu.VMEM((blocks, side, side), bf16),
        pltpu.VMEM((nb, side, wide), bf16),
        pltpu.SemaphoreType.DMA((nb,)),
    ]
    product_scratch = pltpu.VMEM((wide, blocks * side), bf16)
    left_scratch = [
        pltpu.VMEM((blocks, envs * half, side), bf16),
        pltpu.VMEM((16 * blocks, half, side), bf16),
    ]
    state_flops = 2 * blocks * side * side * wide
    left_flops = 2 * envs * half * wide * blocks * side

    near_flops = left_flops * near // envs
    core_index = jnp.broadcast_to(core, (1,)).astype(jnp.int32)
    product, partial_near = pl.pallas_call(
        product_kernel,
        out_shape=[
            jax.ShapeDtypeStruct((wide, blocks * side), bf16),
            jax.ShapeDtypeStruct((blocks, near * half, side), bf16),
        ],
        in_specs=[smem] + [vmem] * 3 + [anywhere] + [vmem] * 3,
        out_specs=[vmem] * 2,
        scratch_shapes=state_scratch,
        compiler_params=params(22),
        cost_estimate=pl.CostEstimate(
            flops=state_flops + near_flops, bytes_accessed=0, transcendentals=0
        ),
        name="product",
    )(core_index, own_rows, other_rows, *rights, own, below, above)

    for step in range(2):
        if step == 0:
            *sums, left = pl.pallas_call(
                first_kernel,
                out_shape=sums_shape + [jax.ShapeDtypeStruct(left_shape, bf16)],
                in_specs=[smem] * 2 + [vmem] * 9,
                out_specs=[vmem] * 5,
                scratch_shapes=left_scratch + [
                    pltpu.SemaphoreType.DMA((16,)), pltpu.SemaphoreType.DMA((near,))
                ],
                compiler_params=params(16),
                cost_estimate=pl.CostEstimate(
                    flops=left_flops - near_flops, bytes_accessed=0, transcendentals=0
                ),
                name="contract_first",
            )(pairs, places, own, below, above, *parts, product, partial_near)
        else:
            sums = pl.pallas_call(
                second_kernel,
                out_shape=sums_shape,
                in_specs=[smem] + [vmem] * 3 + [anywhere, vmem],
                out_specs=[vmem] * 4,
                scratch_shapes=state_scratch + [product_scratch] + left_scratch,
                compiler_params=params(30),
                cost_estimate=pl.CostEstimate(
                    flops=left_flops + state_flops, bytes_accessed=0, transcendentals=0
                ),
                name="contract_second",
            )(pairs, own_rows, other_rows, *rights, left)
        got = [send(sums[k + 1], first(d)) for k, d in enumerate(shifts)]
        summed = sums[0].astype(f32)
        for g in got:
            summed = summed + g.astype(f32)
        summed = summed.astype(bf16).reshape(4, blocks, half, side)
        got = [send(summed[k + 1], second(d)) for k, d in enumerate(shifts)]
        gradient = summed[0].astype(f32)
        for g in got:
            gradient = gradient + g.astype(f32)
        own_rows = (own_rows.astype(f32) - step_size * gradient).astype(bf16)
        if step == 0:
            other_rows = send(own_rows, swap_cores)
    keep = jnp.where(lower, own_rows[:nb], own_rows[nb:])
    give = jnp.where(lower, own_rows[nb:], own_rows[:nb])
    come = send(give, swap_cores)
    return jnp.concatenate(
        [jnp.where(lower, keep, come), jnp.where(lower, come, keep)], axis=1
    )


def solution(mesh):
    placed = (
        P(("row", "col"), None, None),
        P(("row", "col"), None, None, None),
        P("row", None, None, None),
        P(("row", "col")),
        P(("row", "col")),
        P(("row", "col")),
        P(("row", "col")),
    )
    return jax.shard_map(
        on_device,
        mesh=mesh,
        in_specs=placed,
        out_specs=P(("row", "col"), None, None),
        check_vma=False,
    )
```

```python
import jax
import jax.numpy as jnp
from jax import lax
from jax.experimental import pallas as pl
from jax.experimental.pallas import tpu as pltpu
from jax.sharding import PartitionSpec as P

step_size = 0.3
NZ, NY, NX = 8, 4, 4
axes = ("row", "col")

far = (2, -2, 3, -3, 4)
thirds = 3
third_w = 11
near = 3


def device(z, y, x, c):
    return ((z % NZ * NY + y % NY) * NX + x % NX) * 2 + c


def permutation(to):
    return [
        (device(z, y, x, c), device(*to(z, y, x, c)))
        for z in range(NZ) for y in range(NY) for x in range(NX) for c in range(2)
    ]


swap_cores = permutation(lambda z, y, x, c: (z, y, x, 1 - c))


def first(d):
    return permutation(lambda z, y, x, c: (z, y, x + d, c) if c == 0 else (z, y + d, x, c))


def second(d):
    return permutation(lambda z, y, x, c: (z, y + d, x, c) if c == 0 else (z, y, x + d, c))


def along_z(d):
    return permutation(lambda z, y, x, c: (z + d, y, x, c))


def fetch_place(z, y, x, c):
    group = min((y * NX + x) // thirds, len(far) - 1)
    d = far[group] if c == 0 else -far[group]
    return z - d, y, x, c


fetch_far = permutation(fetch_place)
shifts = (1, 2, -1)


def send(a, perm):
    return lax.ppermute(a, axes, perm)


def table(values, index):
    out = jnp.full_like(index, values[0])
    for k, v in enumerate(values[1:], 1):
        out = jnp.where(index == k, v, out)
    return out


vmem = pl.BlockSpec(memory_space=pltpu.VMEM)
smem = pl.BlockSpec(memory_space=pltpu.SMEM)
anywhere = pl.BlockSpec(memory_space=pl.ANY)


def params(mib):
    return pltpu.CompilerParams(vmem_limit_bytes=mib * 1024 * 1024)


def multiply_state(
    core, own_rows, other_rows, right_own, right_other, right_v, right_sems, state, product
):
    count, side, wide = right_own.shape
    copies = [
        pltpu.make_async_copy(right_other.at[b], right_v.at[b], right_sems.at[b])
        for b in range(count)
    ]
    for c in copies:
        c.start()
    half = side // 2
    blocks = state.shape[0]
    nb = blocks // 2
    mine = pl.multiple_of(core * half, half)
    theirs = pl.multiple_of((1 - core) * half, half)
    state[:, pl.ds(mine, half), :] = own_rows[...]
    state[:, pl.ds(theirs, half), :] = other_rows[...]
    step = 512
    for b in range(blocks):
        at = core * nb + b if b < nb else (1 - core) * nb + b - nb
        if b >= count:
            copies[b - count].wait()
        right = right_own.at[b] if b < count else right_v.at[b - count]
        s = state[at]
        for n in range(wide // step):
            r = jnp.dot(
                s, right[:, n * step:(n + 1) * step], preferred_element_type=jnp.float32
            ).astype(jnp.bfloat16)
            for q in range(step // side):
                w = n * (step // side) + q
                product[w * side:(w + 1) * side, b * side:(b + 1) * side] = r[
                    :, q * side:(q + 1) * side
                ]


def multiply_left(left, product, partial, start, stop):
    wide = product.shape[0]
    side = partial.shape[2]
    for n in range(partial.shape[0] // 2):
        r = jnp.dot(
            left[:, :wide], product[:, n * 2 * side:(n + 1) * 2 * side],
            preferred_element_type=jnp.float32,
        ).astype(jnp.bfloat16)
        partial[2 * n, start:stop] = r[:, :side]
        partial[2 * n + 1, start:stop] = r[:, side:]


def place_pairs(pairs, partial, total, outs):
    half = total.shape[1]

    def place(p, carry):
        at = pl.multiple_of(pairs[0, p] * half, half)
        to = pairs[2, p]
        value = partial[pairs[1, p], pl.ds(at, half), :].astype(jnp.float32)
        total[to] = (total[to].astype(jnp.float32) + value).astype(jnp.bfloat16)
        return carry

    lax.fori_loop(0, pairs.shape[1], place, 0, unroll=4)
    count = outs[0].shape[0]
    for i, out in enumerate(outs):
        out[...] = total[i * count:(i + 1) * count]


def product_kernel(
    core, own_rows, other_rows, right_own, right_other, own, below, above,
    product, partial, state, right_v, right_sems,
):
    multiply_state(
        core[0], own_rows, other_rows, right_own, right_other, right_v, right_sems, state, product
    )
    stacked = jnp.concatenate([own[...], below[...], above[...]], axis=0)
    multiply_left(stacked, product, partial, 0, stacked.shape[0])


def first_kernel(
    pairs, places, own, below, above, part0, part1, part2, part3, product, partial_near,
    out0, out1, out2, out3, left, partial, total, sems, near_sems,
):
    half, wide = own.shape
    near_rows = near * half
    rows = partial.shape[1]
    near_copies = [
        pltpu.make_async_copy(
            ref, left.at[i * half:(i + 1) * half, 0:wide], near_sems.at[i]
        )
        for i, ref in enumerate((own, below, above))
    ]
    copies = []
    for i, ref in enumerate((part0, part1, part2, part3)):
        for j in range(4):
            row = pl.multiple_of(places[0, i * 4 + j], half)
            column = pl.multiple_of(places[1, i * 4 + j], 128)
            copies.append(
                pltpu.make_async_copy(
                    ref.at[j], left.at[pl.ds(row, half), pl.ds(column, ref.shape[2])],
                    sems.at[i * 4 + j],
                )
            )
    for c in copies + near_copies:
        c.start()
    total[...] = jnp.zeros_like(total)
    partial[:, :near_rows] = partial_near[...]
    for c in copies + near_copies:
        c.wait()
    multiply_left(left.at[near_rows:rows], product, partial, near_rows, rows)
    place_pairs(pairs, partial, total, (out0, out1, out2, out3))


def second_kernel(
    pairs, own_rows, other_rows, right_own, right_other, left,
    out0, out1, out2, out3, state, right_v, right_sems, product, partial, total,
):
    rows = partial.shape[1]
    total[...] = jnp.zeros_like(total)
    multiply_state(
        pairs[3, 0], own_rows, other_rows, right_own, right_other, right_v, right_sems, state, product
    )
    multiply_left(left.at[:rows], product, partial, 0, rows)
    place_pairs(pairs, partial, total, (out0, out1, out2, out3))


def on_device(psi, right_env, left_env, env_index, source_block, target_slot, target_block):
    nb, side, width, _ = right_env.shape
    half = side // 2
    blocks = 2 * nb
    envs = NZ
    wide = width * side
    third = third_w * side
    bf16, f32 = jnp.bfloat16, jnp.float32
    z = lax.axis_index("row")
    col = lax.axis_index("col")
    core, x, y = col % 2, col // 2 % NX, col // (2 * NX)
    lower = core == 0
    chip = y * NX + x

    own = lax.dynamic_slice_in_dim(left_env[0], core * half, half, 0).reshape(half, wide)
    padded = jnp.pad(own, ((0, 0), (0, thirds * third - wide)))
    mine = lax.dynamic_slice_in_dim(padded, chip % thirds * third, third, 1)
    held = send(mine, fetch_far)
    right_env, _ = lax.optimization_barrier((right_env, mine))
    right_own = right_env.reshape(nb, side, wide)
    psi_other = send(psi, swap_cores)
    held, own, right_own, psi_other = lax.optimization_barrier((held, own, right_own, psi_other))
    right_other = send(right_own, swap_cores)
    below = send(own, along_z(1))
    above = send(own, along_z(-1))
    line = jnp.stack([held] + [send(held, first(d)) for d in shifts])
    line, right_other = lax.optimization_barrier((line, right_other))
    last_line, below, above, env_index, target_slot = lax.optimization_barrier(
        (line, below, above, env_index, target_slot)
    )
    offset = (env_index - z) % envs
    slot_lower = table([0, 2, 3, 5, 7, 6, 4, 1], offset)
    slot_upper = table([0, 2, 4, 6, 7, 5, 3, 1], offset)
    owner = target_slot // 2
    to_y, to_x, to_c = owner // (2 * NX), owner // 2 % NX, owner % 2
    ry, rx = (to_y - y) % NY, (to_x - x) % NX
    block = to_c * nb + target_block
    x_first = (rx * 4 + ry) * blocks + block
    y_first = (ry * 4 + rx) * blocks + block
    lists = jnp.stack([slot_lower, slot_upper, source_block, x_first, y_first])
    their_lists = send(lists, swap_cores)
    parts = [line] + [send(last_line if d < 0 else line, second(d)) for d in shifts]
    rights = (right_own, right_other)

    back = jnp.array([0, -1, -2, 1], jnp.int32)
    by_first, by_second = back[None, :], back[:, None]
    px = (x + jnp.where(lower, by_first, by_second)) % NX
    py = (y + jnp.where(lower, by_second, by_first)) % NY
    at = (py * NX + px).reshape(-1)
    places = jnp.stack([(near + at // thirds) * half, at % thirds * third])

    theirs = their_lists + jnp.array([[0], [0], [nb], [0], [0]], jnp.int32)
    both = jnp.concatenate([lists, theirs], axis=1)
    pairs = jnp.stack([
        jnp.where(lower, both[0], both[1]), both[2],
        jnp.where(lower, both[3], both[4]), jnp.broadcast_to(core, both[2].shape),
    ])

    state = jnp.concatenate(
        [jnp.where(lower, psi, psi_other), jnp.where(lower, psi_other, psi)], axis=0
    )
    own_rows = jnp.where(lower, state[:, :half], state[:, half:])
    other_rows = jnp.where(lower, state[:, half:], state[:, :half])

    pair_count = pairs.shape[1]
    left_shape = ((envs + 1) * half, thirds * third)
    sums_shape = [jax.ShapeDtypeStruct((4 * blocks, half, side), bf16)] * 4
    state_scratch = [
        pltpu.VMEM((blocks, side, side), bf16),
        pltpu.VMEM((nb, side, wide), bf16),
        pltpu.SemaphoreType.DMA((nb,)),
    ]
    product_scratch = pltpu.VMEM((wide, blocks * side), bf16)
    left_scratch = [
        pltpu.VMEM((blocks, envs * half, side), bf16),
        pltpu.VMEM((16 * blocks, half, side), bf16),
    ]
    state_flops = 2 * blocks * side * side * wide
    left_flops = 2 * envs * half * wide * blocks * side

    near_flops = left_flops * near // envs
    core_index = jnp.broadcast_to(core, (1,)).astype(jnp.int32)
    product, partial_near = pl.pallas_call(
        product_kernel,
        out_shape=[
            jax.ShapeDtypeStruct((wide, blocks * side), bf16),
            jax.ShapeDtypeStruct((blocks, near * half, side), bf16),
        ],
        in_specs=[smem] + [vmem] * 3 + [anywhere] + [vmem] * 3,
        out_specs=[vmem] * 2,
        scratch_shapes=state_scratch,
        compiler_params=params(22),
        cost_estimate=pl.CostEstimate(
            flops=state_flops + near_flops, bytes_accessed=0, transcendentals=0
        ),
        name="product",
    )(core_index, own_rows, other_rows, *rights, own, below, above)

    for step in range(2):
        if step == 0:
            *sums, left = pl.pallas_call(
                first_kernel,
                out_shape=sums_shape + [jax.ShapeDtypeStruct(left_shape, bf16)],
                in_specs=[smem] * 2 + [vmem] * 9,
                out_specs=[vmem] * 5,
                scratch_shapes=left_scratch + [
                    pltpu.SemaphoreType.DMA((16,)), pltpu.SemaphoreType.DMA((near,))
                ],
                compiler_params=params(16),
                cost_estimate=pl.CostEstimate(
                    flops=left_flops - near_flops, bytes_accessed=0, transcendentals=0
                ),
                name="contract_first",
            )(pairs, places, own, below, above, *parts, product, partial_near)
        else:
            sums = pl.pallas_call(
                second_kernel,
                out_shape=sums_shape,
                in_specs=[smem] + [vmem] * 3 + [anywhere, vmem],
                out_specs=[vmem] * 4,
                scratch_shapes=state_scratch + [product_scratch] + left_scratch,
                compiler_params=params(30),
                cost_estimate=pl.CostEstimate(
                    flops=left_flops + state_flops, bytes_accessed=0, transcendentals=0
                ),
                name="contract_second",
            )(pairs, own_rows, other_rows, *rights, left)
        got = [send(sums[k + 1], first(d)) for k, d in enumerate(shifts)]
        summed = sums[0].astype(f32)
        for g in got:
            summed = summed + g.astype(f32)
        summed = summed.astype(bf16).reshape(4, blocks, half, side)
        got = [send(summed[k + 1], second(d)) for k, d in enumerate(shifts)]
        gradient = summed[0].astype(f32)
        for g in got:
            gradient = gradient + g.astype(f32)
        own_rows = (own_rows.astype(f32) - step_size * gradient).astype(bf16)
        if step == 0:
            other_rows = send(own_rows, swap_cores)
    keep = jnp.where(lower, own_rows[:nb], own_rows[nb:])
    give = jnp.where(lower, own_rows[nb:], own_rows[:nb])
    come = send(give, swap_cores)
    return jnp.concatenate(
        [jnp.where(lower, keep, come), jnp.where(lower, come, keep)], axis=1
    )


def solution(mesh):
    placed = (
        P(("row", "col"), None, None),
        P(("row", "col"), None, None, None),
        P("row", None, None, None),
        P(("row", "col")),
        P(("row", "col")),
        P(("row", "col")),
        P(("row", "col")),
    )
    return jax.shard_map(
        on_device,
        mesh=mesh,
        in_specs=placed,
        out_specs=P(("row", "col"), None, None),
        check_vma=False,
    )
```

```python
import jax
import jax.numpy as jnp
from jax import lax
from jax.experimental import pallas as pl
from jax.experimental.pallas import tpu as pltpu
from jax.sharding import PartitionSpec as P

step_size = 0.3
NZ, NY, NX = 8, 4, 4
axes = ("row", "col")

far = (2, -2, 3, -3, 4)
thirds = 3
third_w = 11
near = 3


def device(z, y, x, c):
    return ((z % NZ * NY + y % NY) * NX + x % NX) * 2 + c


def permutation(to):
    return [
        (device(z, y, x, c), device(*to(z, y, x, c)))
        for z in range(NZ) for y in range(NY) for x in range(NX) for c in range(2)
    ]


swap_cores = permutation(lambda z, y, x, c: (z, y, x, 1 - c))


def first(d):
    return permutation(lambda z, y, x, c: (z, y, x + d, c) if c == 0 else (z, y + d, x, c))


def second(d):
    return permutation(lambda z, y, x, c: (z, y + d, x, c) if c == 0 else (z, y, x + d, c))


def along_z(d):
    return permutation(lambda z, y, x, c: (z + d, y, x, c))


def fetch_place(z, y, x, c):
    group = min((y * NX + x) // thirds, len(far) - 1)
    d = far[group] if c == 0 else -far[group]
    return z - d, y, x, c


fetch_far = permutation(fetch_place)
shifts = (1, 2, -1)


def send(a, perm):
    return lax.ppermute(a, axes, perm)


def table(values, index):
    out = jnp.full_like(index, values[0])
    for k, v in enumerate(values[1:], 1):
        out = jnp.where(index == k, v, out)
    return out


vmem = pl.BlockSpec(memory_space=pltpu.VMEM)
smem = pl.BlockSpec(memory_space=pltpu.SMEM)
anywhere = pl.BlockSpec(memory_space=pl.ANY)


def params(mib):
    return pltpu.CompilerParams(vmem_limit_bytes=mib * 1024 * 1024)


def multiply_state(
    core, own_rows, other_rows, right_own, right_other, right_v, right_sems, state, product
):
    count, side, wide = right_own.shape
    copies = [
        pltpu.make_async_copy(right_other.at[b], right_v.at[b], right_sems.at[b])
        for b in range(count)
    ]
    for c in copies:
        c.start()
    half = side // 2
    blocks = state.shape[0]
    nb = blocks // 2
    mine = pl.multiple_of(core * half, half)
    theirs = pl.multiple_of((1 - core) * half, half)
    state[:, pl.ds(mine, half), :] = own_rows[...]
    state[:, pl.ds(theirs, half), :] = other_rows[...]
    step = 512
    for b in range(blocks):
        at = core * nb + b if b < nb else (1 - core) * nb + b - nb
        if b >= count:
            copies[b - count].wait()
        right = right_own.at[b] if b < count else right_v.at[b - count]
        s = state[at]
        for n in range(wide // step):
            r = jnp.dot(
                s, right[:, n * step:(n + 1) * step], preferred_element_type=jnp.float32
            ).astype(jnp.bfloat16)
            for q in range(step // side):
                w = n * (step // side) + q
                product[w * side:(w + 1) * side, b * side:(b + 1) * side] = r[
                    :, q * side:(q + 1) * side
                ]


def multiply_left(left, product, partial, start, stop):
    wide = product.shape[0]
    side = partial.shape[2]
    for n in range(partial.shape[0] // 2):
        r = jnp.dot(
            left[:, :wide], product[:, n * 2 * side:(n + 1) * 2 * side],
            preferred_element_type=jnp.float32,
        ).astype(jnp.bfloat16)
        partial[2 * n, start:stop] = r[:, :side]
        partial[2 * n + 1, start:stop] = r[:, side:]


def place_pairs(pairs, partial, total, outs):
    half = total.shape[1]

    def place(p, carry):
        at = pl.multiple_of(pairs[0, p] * half, half)
        to = pairs[2, p]
        value = partial[pairs[1, p], pl.ds(at, half), :].astype(jnp.float32)
        total[to] = (total[to].astype(jnp.float32) + value).astype(jnp.bfloat16)
        return carry

    lax.fori_loop(0, pairs.shape[1], place, 0, unroll=4)
    count = outs[0].shape[0]
    for i, out in enumerate(outs):
        out[...] = total[i * count:(i + 1) * count]


def product_kernel(
    core, own_rows, other_rows, right_own, right_other, own, below, above,
    product, partial, state, right_v, right_sems,
):
    multiply_state(
        core[0], own_rows, other_rows, right_own, right_other, right_v, right_sems, state, product
    )
    stacked = jnp.concatenate([own[...], below[...], above[...]], axis=0)
    multiply_left(stacked, product, partial, 0, stacked.shape[0])


def first_kernel(
    pairs, places, own, below, above, part0, part1, part2, part3, product, partial_near,
    out0, out1, out2, out3, left, partial, total, sems, near_sems,
):
    half, wide = own.shape
    near_rows = near * half
    rows = partial.shape[1]
    near_copies = [
        pltpu.make_async_copy(
            ref, left.at[i * half:(i + 1) * half, 0:wide], near_sems.at[i]
        )
        for i, ref in enumerate((own, below, above))
    ]
    copies = []
    for i, ref in enumerate((part0, part1, part2, part3)):
        for j in range(4):
            row = pl.multiple_of(places[0, i * 4 + j], half)
            column = pl.multiple_of(places[1, i * 4 + j], 128)
            copies.append(
                pltpu.make_async_copy(
                    ref.at[j], left.at[pl.ds(row, half), pl.ds(column, ref.shape[2])],
                    sems.at[i * 4 + j],
                )
            )
    for c in copies + near_copies:
        c.start()
    total[...] = jnp.zeros_like(total)
    partial[:, :near_rows] = partial_near[...]
    for c in copies + near_copies:
        c.wait()
    multiply_left(left.at[near_rows:rows], product, partial, near_rows, rows)
    place_pairs(pairs, partial, total, (out0, out1, out2, out3))


def second_kernel(
    pairs, own_rows, other_rows, right_own, right_other, left,
    out0, out1, out2, out3, state, right_v, right_sems, product, partial, total,
):
    rows = partial.shape[1]
    total[...] = jnp.zeros_like(total)
    multiply_state(
        pairs[3, 0], own_rows, other_rows, right_own, right_other, right_v, right_sems, state, product
    )
    multiply_left(left.at[:rows], product, partial, 0, rows)
    place_pairs(pairs, partial, total, (out0, out1, out2, out3))


def on_device(psi, right_env, left_env, env_index, source_block, target_slot, target_block):
    nb, side, width, _ = right_env.shape
    half = side // 2
    blocks = 2 * nb
    envs = NZ
    wide = width * side
    third = third_w * side
    bf16, f32 = jnp.bfloat16, jnp.float32
    z = lax.axis_index("row")
    col = lax.axis_index("col")
    core, x, y = col % 2, col // 2 % NX, col // (2 * NX)
    lower = core == 0
    chip = y * NX + x

    own = lax.dynamic_slice_in_dim(left_env[0], core * half, half, 0).reshape(half, wide)
    padded = jnp.pad(own, ((0, 0), (0, thirds * third - wide)))
    mine = lax.dynamic_slice_in_dim(padded, chip % thirds * third, third, 1)
    held = send(mine, fetch_far)
    env_index, target_slot, right_env, _ = lax.optimization_barrier(
        (env_index, target_slot, right_env, mine)
    )
    offset = (env_index - z) % envs
    slot_lower = table([0, 2, 3, 5, 7, 6, 4, 1], offset)
    slot_upper = table([0, 2, 4, 6, 7, 5, 3, 1], offset)
    owner = target_slot // 2
    to_y, to_x, to_c = owner // (2 * NX), owner // 2 % NX, owner % 2
    ry, rx = (to_y - y) % NY, (to_x - x) % NX
    block = to_c * nb + target_block
    x_first = (rx * 4 + ry) * blocks + block
    y_first = (ry * 4 + rx) * blocks + block
    lists = jnp.stack([slot_lower, slot_upper, source_block, x_first, y_first])
    right_own = right_env.reshape(nb, side, wide)
    psi_other = send(psi, swap_cores)
    their_lists = send(lists, swap_cores)
    held, own, right_own, psi_other, their_lists = lax.optimization_barrier(
        (held, own, right_own, psi_other, their_lists)
    )
    right_other = send(right_own, swap_cores)
    below = send(own, along_z(1))
    above = send(own, along_z(-1))
    line = jnp.stack([held] + [send(held, first(d)) for d in shifts])
    line, right_other = lax.optimization_barrier((line, right_other))
    last_line, below, above = lax.optimization_barrier((line, below, above))
    parts = [line] + [send(last_line if d < 0 else line, second(d)) for d in shifts]
    rights = (right_own, right_other)

    back = jnp.array([0, -1, -2, 1], jnp.int32)
    by_first, by_second = back[None, :], back[:, None]
    px = (x + jnp.where(lower, by_first, by_second)) % NX
    py = (y + jnp.where(lower, by_second, by_first)) % NY
    at = (py * NX + px).reshape(-1)
    places = jnp.stack([(near + at // thirds) * half, at % thirds * third])

    theirs = their_lists + jnp.array([[0], [0], [nb], [0], [0]], jnp.int32)
    both = jnp.concatenate([lists, theirs], axis=1)
    pairs = jnp.stack([
        jnp.where(lower, both[0], both[1]), both[2],
        jnp.where(lower, both[3], both[4]), jnp.broadcast_to(core, both[2].shape),
    ])

    state = jnp.concatenate(
        [jnp.where(lower, psi, psi_other), jnp.where(lower, psi_other, psi)], axis=0
    )
    own_rows = jnp.where(lower, state[:, :half], state[:, half:])
    other_rows = jnp.where(lower, state[:, half:], state[:, :half])

    pair_count = pairs.shape[1]
    left_shape = ((envs + 1) * half, thirds * third)
    sums_shape = [jax.ShapeDtypeStruct((4 * blocks, half, side), bf16)] * 4
    state_scratch = [
        pltpu.VMEM((blocks, side, side), bf16),
        pltpu.VMEM((nb, side, wide), bf16),
        pltpu.SemaphoreType.DMA((nb,)),
    ]
    product_scratch = pltpu.VMEM((wide, blocks * side), bf16)
    left_scratch = [
        pltpu.VMEM((blocks, envs * half, side), bf16),
        pltpu.VMEM((16 * blocks, half, side), bf16),
    ]
    state_flops = 2 * blocks * side * side * wide
    left_flops = 2 * envs * half * wide * blocks * side

    near_flops = left_flops * near // envs
    core_index = jnp.broadcast_to(core, (1,)).astype(jnp.int32)
    product, partial_near = pl.pallas_call(
        product_kernel,
        out_shape=[
            jax.ShapeDtypeStruct((wide, blocks * side), bf16),
            jax.ShapeDtypeStruct((blocks, near * half, side), bf16),
        ],
        in_specs=[smem] + [vmem] * 3 + [anywhere] + [vmem] * 3,
        out_specs=[vmem] * 2,
        scratch_shapes=state_scratch,
        compiler_params=params(22),
        cost_estimate=pl.CostEstimate(
            flops=state_flops + near_flops, bytes_accessed=0, transcendentals=0
        ),
        name="product",
    )(core_index, own_rows, other_rows, *rights, own, below, above)

    for step in range(2):
        if step == 0:
            *sums, left = pl.pallas_call(
                first_kernel,
                out_shape=sums_shape + [jax.ShapeDtypeStruct(left_shape, bf16)],
                in_specs=[smem] * 2 + [vmem] * 9,
                out_specs=[vmem] * 5,
                scratch_shapes=left_scratch + [
                    pltpu.SemaphoreType.DMA((16,)), pltpu.SemaphoreType.DMA((near,))
                ],
                compiler_params=params(16),
                cost_estimate=pl.CostEstimate(
                    flops=left_flops - near_flops, bytes_accessed=0, transcendentals=0
                ),
                name="contract_first",
            )(pairs, places, own, below, above, *parts, product, partial_near)
        else:
            sums = pl.pallas_call(
                second_kernel,
                out_shape=sums_shape,
                in_specs=[smem] + [vmem] * 3 + [anywhere, vmem],
                out_specs=[vmem] * 4,
                scratch_shapes=state_scratch + [product_scratch] + left_scratch,
                compiler_params=params(30),
                cost_estimate=pl.CostEstimate(
                    flops=left_flops + state_flops, bytes_accessed=0, transcendentals=0
                ),
                name="contract_second",
            )(pairs, own_rows, other_rows, *rights, left)
        got = [send(sums[k + 1], first(shifts[k])) for k in (1, 0, 2)]
        summed = sums[0].astype(f32)
        for g in got:
            summed = summed + g.astype(f32)
        summed = summed.astype(bf16).reshape(4, blocks, half, side)
        got = [send(summed[k + 1], second(shifts[k])) for k in (1, 0, 2)]
        gradient = summed[0].astype(f32)
        for g in got:
            gradient = gradient + g.astype(f32)
        own_rows = (own_rows.astype(f32) - step_size * gradient).astype(bf16)
        if step == 0:
            other_rows = send(own_rows, swap_cores)
    keep = jnp.where(lower, own_rows[:nb], own_rows[nb:])
    give = jnp.where(lower, own_rows[nb:], own_rows[:nb])
    come = send(give, swap_cores)
    return jnp.concatenate(
        [jnp.where(lower, keep, come), jnp.where(lower, come, keep)], axis=1
    )


def solution(mesh):
    placed = (
        P(("row", "col"), None, None),
        P(("row", "col"), None, None, None),
        P("row", None, None, None),
        P(("row", "col")),
        P(("row", "col")),
        P(("row", "col")),
        P(("row", "col")),
    )
    return jax.shard_map(
        on_device,
        mesh=mesh,
        in_specs=placed,
        out_specs=P(("row", "col"), None, None),
        check_vma=False,
    )
```
